32 devices in a mesh: rows: 8 (over y, x, core), sub: 4 (over z).
Axes of the slice: x: 2, y: 2, z: 4, core: 2. Of those that a mesh axis runs over, the one named last changes fastest.
Arguments:
- right_sides: float32 [32768, 512], P(('rows', 'sub')), may hold values from -6 to 6
- bases_u: float32 [4, 32768, 256], P(None, ('rows', 'sub')), may hold values from -0.375 to 0.375
- bases_v: float32 [4, 32768, 256], P(None, ('rows', 'sub')), may hold values from -0.046875 to 0.046875
- couple_first: float32 [512, 512], P(('rows', 'sub')), may hold values from -0.25 to 0.25
- couple_second: float32 [1024, 512], P(('rows', 'sub')), may hold values from -0.25 to 0.25
- couple_third: float32 [2048, 512], P(('rows', 'sub')), may hold values from -0.25 to 0.25
- couple_fourth: float32 [4096, 512], P(('rows', 'sub')), may hold values from -0.25 to 0.25
Outputs:
- solved: float32 [32768, 512], P(('rows', 'sub'))
The draws below stay inside these ranges and needn't reach their ends.
All inputs are finite; a program needn't handle non-finite values.
Results may differ from the reference program's by a relative error of at most 0.00013.
Values sent between devices are 32-bit elements; how exact they have to be, the bound alone decides.
No kernel may reach another device: no remote copies, remote signals or barrier semaphores. Data moves between devices by JAX's collectives and lax.ppermute only.
A program may use at most 64 MiB of HBM per device.

```python
import jax
import jax.numpy as jnp
from jax import lax

RANK = 256
SIDES = 512
LEVELS = 4
ORDER = 32768


def block_levels(own_key, extent, pieces, smallest, largest):
    loudness, own = 1.0, jax.random.fold_in(own_key, 6)
    for dim, shards_of in pieces:
        heights = jnp.exp(jax.random.uniform(jax.random.fold_in(own, dim), (shards_of,), jnp.float32, smallest / len(pieces), largest / len(pieces)))
        loudness = loudness * jnp.repeat(heights, extent[dim] // shards_of).reshape([-1 if axis == dim else 1 for axis in range(len(extent))])
    return loudness


def gaussian(stream_key, extent, spread, most, split=(), kind=jnp.bfloat16):
    level = block_levels(stream_key, extent, split, -0.22, 0.18) if split else 1.0
    drawn = jax.random.normal(stream_key, extent, jnp.float32) * spread * level
    return jnp.minimum(jnp.maximum(drawn, -most), most).astype(kind)


def setup_inputs(seed: int = 0) -> dict:
    arg_keys = jax.random.split(jax.random.key(seed), 8)
    right_sides = gaussian(arg_keys[0], (ORDER, SIDES), 1.0, 6.0, ((0, 32),), jnp.float32)
    bases_u = gaussian(arg_keys[1], (LEVELS, ORDER, RANK), RANK ** -0.5, 0.375, ((1, 32),), jnp.float32)
    bases_v = gaussian(arg_keys[2], (LEVELS, ORDER, RANK), (ORDER // 2) ** -0.5, 0.046875, ((1, 32),), jnp.float32)
    couple_first = gaussian(arg_keys[3], (2 * RANK, 2 * RANK), (2 * RANK) ** -0.5, 0.25, ((0, 32),), jnp.float32)
    couple_second = gaussian(arg_keys[4], (4 * RANK, 2 * RANK), (2 * RANK) ** -0.5, 0.25, ((0, 32),), jnp.float32)
    couple_third = gaussian(arg_keys[5], (8 * RANK, 2 * RANK), (2 * RANK) ** -0.5, 0.25, ((0, 32),), jnp.float32)
    couple_fourth = gaussian(arg_keys[6], (16 * RANK, 2 * RANK), (2 * RANK) ** -0.5, 0.25, ((0, 32),), jnp.float32)
    return {"right_sides": right_sides, "bases_u": bases_u, "bases_v": bases_v, "couple_first": couple_first, "couple_second": couple_second, "couple_third": couple_third, "couple_fourth": couple_fourth}


def reference(right_sides, bases_u, bases_v, couple_first, couple_second, couple_third, couple_fourth):
    couples = (couple_first, couple_second, couple_third, couple_fourth)
    solved = right_sides
    for depth_index in range(LEVELS):
        nodes = 2 ** depth_index
        child_rows = ORDER // (2 * nodes)
        blocks = solved.reshape(2 * nodes, child_rows, SIDES)
        right_blocks = bases_v[depth_index].reshape(2 * nodes, child_rows, RANK)
        sums = jnp.einsum("cnr,cnk->crk", right_blocks, blocks, precision=lax.Precision.HIGHEST)
        paired = sums.reshape(nodes, 2 * RANK, SIDES)
        inverses = couples[depth_index].reshape(nodes, 2 * RANK, 2 * RANK)
        factors = jnp.einsum("nij,njk->nik", inverses, paired, precision=lax.Precision.HIGHEST)
        factors = factors.reshape(2 * nodes, RANK, SIDES)
        left_blocks = bases_u[depth_index].reshape(2 * nodes, child_rows, RANK)
        update = jnp.einsum("cnr,crk->cnk", left_blocks, factors, precision=lax.Precision.HIGHEST)
        solved = solved - update.reshape(ORDER, SIDES)
    return solved
```

```python
import jax
import jax.numpy as jnp
from jax import lax
from jax.sharding import PartitionSpec as P

HIGH = lax.Precision.HIGH
CHUNKS = 1


def dot(left, right, left_dim, right_dim):
    return lax.dot_general(
        left, right, (((left_dim,), (right_dim,)), ((), ())), precision=HIGH, preferred_element_type=jnp.float32
    )


def bits_of(axis):
    return lax.axis_size(axis).bit_length() - 1


def swap(value, place):
    sub_bits = bits_of("sub")
    axis, bit = ("sub", place) if place < sub_bits else ("rows", place - sub_bits)
    return lax.ppermute(value, axis, [(i, i ^ 1 << bit) for i in range(lax.axis_size(axis))])


def digit(place):
    position = lax.axis_index("rows") * lax.axis_size("sub") + lax.axis_index("sub")
    return (position >> place) & 1


def halve(value, dim, place):
    first, second = jnp.split(value, 2, dim)
    lower = digit(place) == 0
    return jnp.where(lower, first, second) + swap(jnp.where(lower, second, first), place)


def ordered(own, other, dim, place):
    lower = digit(place) == 0
    return jnp.where(lower, jnp.concatenate([own, other], dim), jnp.concatenate([other, own], dim))


def widen(value, dim, place):
    return ordered(value, swap(value, place), dim, place)


def common_places(count):
    sub_bits = bits_of("sub")
    places = list(range(count))
    if count > sub_bits:
        places.remove(sub_bits)
        places.insert(0, sub_bits)
    return places


def gram(upper_u, lower_v, places, sibling_place):
    value = dot(lower_v, upper_u, 0, 0)
    for place in places:
        value = halve(value, 0, place)
    for place in reversed(places):
        value = widen(value, 0, place)
    return value, swap(value, sibling_place)


def level_pair(sums, grams, coupling, coupling_next, places, sibling_place):
    rank = sums.shape[2]
    for place in places:
        sums = halve(sums, 1, place)
    other = swap(sums, sibling_place)
    upper = sums[0] + other[0]
    pair = ordered(upper, swap(upper, sibling_place + 1), 1, sibling_place + 1)
    factors = dot(pair, coupling, 1, 1)
    own, sibling = (values[1] - dot(factors, each, 1, 1) for values, each in zip((sums, other), grams))
    factors_next = dot(ordered(own, sibling, 1, sibling_place), coupling_next, 1, 1)
    both = jnp.stack([factors, factors_next])
    for place in reversed(places):
        both = widen(both, 1, place)
    return both


def spread(rows, count):
    places = list(range(count))
    for place in places:
        rows = widen(rows, 0, place)
    return rows


def local(right_sides, bases_u, bases_v, couple_first, couple_second, couple_third, couple_fourth):
    couples = (couple_first, couple_second, couple_third, couple_fourth)
    levels = bases_u.shape[0]
    total_bits = bits_of("sub") + bits_of("rows")
    parts = jnp.split(right_sides, CHUNKS, 1)
    for level in range(0, levels, 2):
        sibling_place = total_bits - level - 2
        places = common_places(sibling_place)
        coupling = spread(couples[level], sibling_place + 1)
        coupling_next = spread(couples[level + 1], sibling_place)
        grams = gram(bases_u[level], bases_v[level + 1], places, sibling_place)
        for index, part in enumerate(parts):
            sums = jnp.stack([dot(part, bases_v[level + k], 0, 0) for k in range(2)])
            factors = level_pair(sums, grams, coupling, coupling_next, places, sibling_place)
            for k in range(2):
                part = part - dot(bases_u[level + k], factors[k], 1, 1)
            parts[index] = part
    return jnp.concatenate(parts, 1)


def solution(mesh):
    placed = (
        P(("rows", "sub"), None),
        P(None, ("rows", "sub"), None),
        P(None, ("rows", "sub"), None),
        P(("rows", "sub"), None),
        P(("rows", "sub"), None),
        P(("rows", "sub"), None),
        P(("rows", "sub"), None),
    )
    return jax.shard_map(
        local, mesh=mesh, in_specs=placed, out_specs=P(("rows", "sub"), None), check_vma=False
    )
```

```python
import functools

import jax
import jax.numpy as jnp
from jax import lax
from jax.experimental import pallas as pl
from jax.experimental.pallas import tpu as pltpu
from jax.sharding import PartitionSpec as P

CHUNKS = 2
WHOLE = True
T = (0, 0, 1, 1, 3)
STEPS = 2
MIB = 1 << 20


def bits_of(axis):
    return lax.axis_size(axis).bit_length() - 1


def swap(value, place):
    sub_bits = bits_of("sub")
    axis, bit = ("sub", place) if place < sub_bits else ("rows", place - sub_bits)
    return lax.ppermute(value, axis, [(i, i ^ 1 << bit) for i in range(lax.axis_size(axis))])


def digit(place):
    position = lax.axis_index("rows") * lax.axis_size("sub") + lax.axis_index("sub")
    return (position >> place) & 1


def digits(*places):
    return jnp.stack([digit(place) for place in places]).astype(jnp.int32)


def halve(value, dim, place):
    first, second = jnp.split(value, 2, dim)
    lower = digit(place) == 0
    return jnp.where(lower, first, second) + swap(jnp.where(lower, second, first), place)


def ordered(own, other, dim, place):
    lower = digit(place) == 0
    return jnp.where(lower, jnp.concatenate([own, other], dim), jnp.concatenate([other, own], dim))


def widen(value, dim, place):
    return ordered(value, swap(value, place), dim, place)


def common_places(count):
    sub_bits = bits_of("sub")
    places = list(range(count))
    if count > sub_bits:
        places.remove(sub_bits)
        places.insert(0, sub_bits)
    return places


def swap_all(values, place):
    width = values[0].shape[-1]
    sent = swap(jnp.concatenate([value.reshape(-1, width) for value in values], 0), place)
    ends = [0]
    for value in values:
        ends.append(ends[-1] + value.size // width)
    return [sent[ends[i] : ends[i + 1]].reshape(value.shape) for i, value in enumerate(values)]


def after(value, tokens, index):
    return lax.optimization_barrier((value, tokens[min(index, len(tokens) - 1)]))[0]


def halves(value):
    high = value.astype(jnp.bfloat16)
    return high, (value - high.astype(jnp.float32)).astype(jnp.bfloat16)


def product(left, right, left_dim, right_dim):
    dims = (((left_dim,), (right_dim,)), ((), ()))

    def one(a, b):
        return lax.dot_general(a, b, dims, preferred_element_type=jnp.float32)

    return one(left[0], right[0]) + (one(left[0], right[1]) + one(left[1], right[0]))


def put_sums(keep_ref, send_ref, chunk, at, where, sums):
    width = keep_ref.shape[0]
    del width
    for ref, side in ((keep_ref, where), (send_ref, 1 - where)):
        for level, (total, width) in enumerate(sums):
            start = pl.multiple_of((side * chunk[1] + chunk[0]) * width, width)
            ref[pl.ds(at + level * width, width), :] = total[pl.ds(start, width), :]


def first_kernel(where_ref, x_ref, u_ref, v_ref, v_next_ref, keep_ref, send_ref, total, total_next):
    step = pl.program_id(0)

    @pl.when(step == 0)
    def _():
        total[...] = jnp.zeros_like(total)
        total_next[...] = jnp.zeros_like(total_next)

    sides = x_ref.shape[1]
    x, v, v_next = halves(x_ref[...]), halves(v_ref[0]), halves(v_next_ref[0])
    total[...] += product(x, v, 0, 0)
    total_next[:sides] += product(x, v_next, 0, 0)
    total_next[sides:] += product(halves(u_ref[0]), v_next, 0, 0)

    @pl.when(step == pl.num_programs(0) - 1)
    def _():
        where = where_ref[0]
        width = sides // (2 * CHUNKS)
        for ref, side in ((keep_ref, where), (send_ref, 1 - where)):
            start = pl.multiple_of(side * CHUNKS * width, width)
            ref[: CHUNKS * width, :] = total[pl.ds(start, CHUNKS * width), :]
            ref[CHUNKS * width : 2 * CHUNKS * width, :] = total_next[pl.ds(start, CHUNKS * width), :]
        rank = u_ref.shape[2]
        at = 2 * CHUNKS * width
        for ref, side in ((keep_ref, where), (send_ref, 1 - where)):
            start = pl.multiple_of(sides + side * (rank // 2), rank // 2)
            ref[at:, :] = total_next[pl.ds(start, rank // 2), :]


def slab(rows, rank, level):
    return pl.BlockSpec((1, rows, rank), lambda i, *_: (level, i, 0))


def whole(shape):
    return pl.BlockSpec(shape, lambda *_: (0,) * len(shape))


def shapes(*values):
    return [jax.ShapeDtypeStruct(value, jnp.float32) for value in values]


SMEM = pl.BlockSpec(memory_space=pltpu.SMEM)


def first_sums(where, x, bases_u, bases_v, level):
    rows, sides = x.shape
    rank = bases_u.shape[2]
    block = rows // STEPS
    out = (sides + rank // 2, rank)
    return pl.pallas_call(
        first_kernel,
        grid=(STEPS,),
        in_specs=[
            SMEM,
            pl.BlockSpec((block, sides), lambda i: (i, 0)),
            slab(block, rank, level),
            slab(block, rank, level),
            slab(block, rank, level + 1),
        ],
        out_specs=[whole(out)] * 2,
        out_shape=shapes(out, out),
        scratch_shapes=[pltpu.VMEM((sides, rank), jnp.float32), pltpu.VMEM((sides + rank, rank), jnp.float32)],
        compiler_params=pltpu.CompilerParams(vmem_limit_bytes=60 * MIB),
        cost_estimate=pl.CostEstimate(flops=6 * rows * rank * (2 * sides + rank), bytes_accessed=5 * rows * rank * 4, transcendentals=0),
    )(where, x, bases_u, bases_v, bases_v)


def update(x, u_ref, u_next_ref, factors):
    return x - (
        product(halves(u_ref[0]), halves(factors[0]), 1, 1) + product(halves(u_next_ref[0]), halves(factors[1]), 1, 1)
    )


def middle_kernel(
    where_ref, x0_ref, x1_ref, own_ref, partner_ref, u_ref, u_next_ref, v_ref, v_next_ref, x_ref, keep_ref, send_ref, total, total_next
):
    step = pl.program_id(0)

    @pl.when(step == 0)
    def _():
        total[...] = jnp.zeros_like(total)
        total_next[...] = jnp.zeros_like(total_next)

    own, partner = own_ref[...], partner_ref[...]
    lower = where_ref[0] == 0
    first, second = jnp.where(lower, own, partner), jnp.where(lower, partner, own)
    factors = [jnp.concatenate([first[k], second[k]], 0) for k in range(2)]
    x = update(jnp.concatenate([x0_ref[...], x1_ref[...]], 1), u_ref, u_next_ref, factors)
    x_ref[...] = x
    x = halves(x)
    total[...] += product(x, halves(v_ref[0]), 0, 0)
    total_next[...] += product(x, halves(v_next_ref[0]), 0, 0)

    @pl.when(step == pl.num_programs(0) - 1)
    def _():
        width = x0_ref.shape[1]
        put_sums(keep_ref, send_ref, (0, 1), 0, where_ref[1], ((total, width), (total_next, width)))


def middle(where, chunk, x, own, partner, bases_u, bases_v, level):
    rows, sides = x.shape
    rank = bases_u.shape[2]
    block, width = rows // STEPS, sides // (2 * CHUNKS)
    out = (2 * width, rank)
    return pl.pallas_call(
        middle_kernel,
        grid=(STEPS,),
        in_specs=[
            SMEM,
            pl.BlockSpec((block, width), lambda i: (i, chunk)),
            pl.BlockSpec((block, width), lambda i: (i, CHUNKS + chunk)),
            whole(own.shape),
            whole(own.shape),
            slab(block, rank, level),
            slab(block, rank, level + 1),
            slab(block, rank, level + 2),
            slab(block, rank, level + 3),
        ],
        out_specs=[pl.BlockSpec((block, 2 * width), lambda i: (i, 0)), whole(out), whole(out)],
        out_shape=shapes((rows, 2 * width), out, out),
        scratch_shapes=[pltpu.VMEM((2 * width, rank), jnp.float32)] * 2,
        compiler_params=pltpu.CompilerParams(vmem_limit_bytes=24 * MIB),
        cost_estimate=pl.CostEstimate(flops=24 * rows * rank * width * 2, bytes_accessed=4 * rows * rank * 4, transcendentals=0),
    )(where, x, x, own, partner, bases_u, bases_u, bases_v, bases_v)


def last_kernel(where_ref, x_ref, own_ref, partner_ref, u_ref, u_next_ref, *refs):
    out_ref = refs[-1]
    mine = where_ref[0] == pl.program_id(1)
    factors = jnp.where(mine, own_ref[...], partner_ref[...])
    out_ref[...] = update(x_ref[...], u_ref, u_next_ref, factors)


def last(where, chunk, x, own, partner, bases_u, level, into, sides):
    rows = x.shape[0]
    rank = bases_u.shape[2]
    block, width = rows // STEPS, sides // (2 * CHUNKS)
    more = [] if into is None else [into]
    return pl.pallas_call(
        last_kernel,
        grid=(STEPS, 2),
        in_specs=[
            SMEM,
            pl.BlockSpec((block, width), lambda i, b: (i, b)),
            whole(own.shape),
            whole(own.shape),
            slab(block, rank, level),
            slab(block, rank, level + 1),
        ]
        + [pl.BlockSpec(memory_space=pl.ANY)] * len(more),
        out_specs=pl.BlockSpec((block, width), lambda i, b: (i, CHUNKS * b + chunk)),
        out_shape=jax.ShapeDtypeStruct((rows, sides), jnp.float32),
        input_output_aliases={6: 0} if more else {},
        compiler_params=pltpu.CompilerParams(vmem_limit_bytes=24 * MIB),
        cost_estimate=pl.CostEstimate(flops=12 * rows * rank * width * 2, bytes_accessed=3 * rows * rank * 4, transcendentals=0),
    )(where, x, own, partner, bases_u, bases_u, *more)


def gram_kernel(u_ref, v_ref, out_ref):
    out_ref[...] = product(halves(u_ref[0]), halves(v_ref[0]), 0, 0)


def gram_term(bases_u, bases_v, level):
    rows, rank = bases_u.shape[1:]
    return pl.pallas_call(
        gram_kernel,
        grid=(1,),
        in_specs=[slab(rows, rank, level), slab(rows, rank, level + 1)],
        out_specs=whole((rank, rank)),
        out_shape=jax.ShapeDtypeStruct((rank, rank), jnp.float32),
        compiler_params=pltpu.CompilerParams(vmem_limit_bytes=24 * MIB),
        cost_estimate=pl.CostEstimate(flops=6 * rows * rank * rank, bytes_accessed=2 * rows * rank * 4, transcendentals=0),
    )(bases_u, bases_v)


def first_gram(value, places, sibling_place, tokens, start):
    for place in places[:0:-1]:
        value = after(value, tokens, start)
        value = value + swap(value, place)
        start += 1
    other = swap(after(value, tokens, start), sibling_place)
    both = widen(jnp.stack([value, other]), 1, places[0])
    return both[0], both[1]


def later_gram(value, places, sibling_place, tokens, start):
    for place in places:
        value = after(value, tokens, start)
        value = value + swap(value, place)
        start += 1
    return value, swap(after(value, tokens, start), sibling_place)


def couplings(rows, rows_next, places, sibling_place, tokens, start):
    values = [rows, rows_next]
    seen = [[], []]
    order = places[::-1]
    order.insert(len(order) - 1, sibling_place)
    for step, place in enumerate(order):
        if start + step >= 0:
            values = [after(value, tokens, start + step) for value in values]
        use = (0,) if place == sibling_place else (0, 1)
        grown = []
        for k in use:
            at = sum(other > place for other in seen[k])
            seen[k].append(place)
            grown.append((jnp.expand_dims(values[k], at), at))
        partners = swap_all([value for value, _ in grown], place)
        for k, (value, at), partner in zip(use, grown, partners):
            values[k] = ordered(value, partner, at, place)
    sides = []
    for k, place in ((0, sibling_place + 1), (1, sibling_place)):
        first, second = jnp.split(values[k].reshape(-1, rows.shape[1]), 2, 1)
        lower = digit(place) == 0
        sides.append((jnp.where(lower, first, second), jnp.where(lower, second, first)))
    return sides


def reduce(sums, places, sibling_place):
    tokens = [sums]
    for place in places[1:]:
        sums = halve(sums, 2, place)
        tokens.append(sums)
    other = swap(sums, sibling_place)
    upper = sums[0] + other[0]
    tokens.append(upper)
    upper_other = swap(upper, sibling_place + 1)
    tokens.append(upper_other)
    return (upper, upper_other, sums[1], other[1]), tokens


def factors_kernel(upper, upper_other, own, sibling, k_own, k_sibling, next_own, next_sibling, gram_own, gram_sibling, out_ref):
    def part(ref):
        return halves(ref[...])

    factors = product(part(upper), part(k_own), 1, 1) + product(part(upper_other), part(k_sibling), 1, 1)
    out_ref[0] = factors
    factors = halves(factors)
    own = halves(own[...] - product(factors, part(gram_own), 1, 0))
    sibling = halves(sibling[...] - product(factors, part(gram_sibling), 1, 0))
    out_ref[1] = product(own, part(next_own), 1, 1) + product(sibling, part(next_sibling), 1, 1)


def factors_of(reduced, grams, sides, places):
    count, width, rank = reduced[0].shape
    reduced = [value.reshape(count * width, rank) for value in reduced]
    both = pl.pallas_call(
        factors_kernel,
        out_shape=jax.ShapeDtypeStruct((2, count * width, rank), jnp.float32),
        compiler_params=pltpu.CompilerParams(vmem_limit_bytes=16 * MIB),
        cost_estimate=pl.CostEstimate(flops=36 * count * width * rank * rank, bytes_accessed=6 * rank * rank * 4, transcendentals=0),
    )(*reduced, *sides[0], *sides[1], *grams)
    found = []
    for k in range(count):
        own = both[:, k * width : (k + 1) * width]
        for place in places[:0:-1]:
            own = widen(own, 1, place)
        found.append((own, swap(own, places[0])))
    return found


def local(right_sides, bases_u, bases_v, couple_first, couple_second, couple_third, couple_fourth):
    couples = (couple_first, couple_second, couple_third, couple_fourth)
    sides, rank = right_sides.shape[1], bases_u.shape[2]
    width = sides // (2 * CHUNKS)
    total_bits = bits_of("sub") + bits_of("rows")
    sibling, sibling_next = total_bits - 2, total_bits - 4
    places, places_next = common_places(sibling), common_places(sibling_next)

    keep, send = first_sums(digits(places[0]), right_sides, bases_u, bases_v, 0)
    sums = keep + swap(send, places[0])
    stacked = sums[:sides].reshape(2, CHUNKS, width, rank)
    groups = [stacked] if WHOLE else [stacked[:, k : k + 1] for k in range(CHUNKS)]
    chunks = [reduce(group, places, sibling) for group in groups]
    tokens = chunks[0][1]
    grams = first_gram(sums[sides:], places, sibling, tokens, T[0])
    coupling = couplings(couples[0], couples[1], places, sibling, tokens, T[1])
    term = gram_term(after(bases_u, tokens, T[2]), bases_v, 2)
    grams_next = later_gram(term, places_next, sibling_next, tokens, T[3])
    coupling_next = couplings(couples[2], couples[3], places_next, sibling_next, tokens, T[4])

    found = [pair for values, _ in chunks for pair in factors_of(values, grams, coupling, places)]
    where = digits(places[0], places_next[0])
    parts, chunks = [], []
    for k, (own, partner) in enumerate(found):
        part, keep, send = middle(where, k, right_sides, own, partner, bases_u, bases_v, 0)
        parts.append(part)
        sums = keep + swap(send, places_next[0])
        chunks.append(reduce(sums.reshape(2, 1, width, rank), places_next, sibling_next))
    solved = None
    for k, (values, _) in enumerate(chunks):
        ((own, partner),) = factors_of(values, grams_next, coupling_next, places_next)
        solved = last(digits(places_next[0]), k, parts[k], own, partner, bases_u, 2, solved, sides)
    return solved


def solution(mesh):
    placed = (
        P(("rows", "sub"), None),
        P(None, ("rows", "sub"), None),
        P(None, ("rows", "sub"), None),
        P(("rows", "sub"), None),
        P(("rows", "sub"), None),
        P(("rows", "sub"), None),
        P(("rows", "sub"), None),
    )
    return jax.shard_map(
        local, mesh=mesh, in_specs=placed, out_specs=P(("rows", "sub"), None), check_vma=False
    )
```

```python
import functools

import jax
import jax.numpy as jnp
from jax import lax
from jax.experimental import pallas as pl
from jax.experimental.pallas import tpu as pltpu
from jax.sharding import PartitionSpec as P

CHUNKS = 2
STEPS = 2
MIB = 1 << 20
LOW = -1
MID = 24
LAST = 24


def bits_of(axis):
    return lax.axis_size(axis).bit_length() - 1


def swap(value, place):
    sub_bits = bits_of("sub")
    axis, bit = ("sub", place) if place < sub_bits else ("rows", place - sub_bits)
    return lax.ppermute(value, axis, [(i, i ^ 1 << bit) for i in range(lax.axis_size(axis))])


def digit(place):
    position = lax.axis_index("rows") * lax.axis_size("sub") + lax.axis_index("sub")
    return (position >> place) & 1


def digits(*places):
    return jnp.stack([digit(place) for place in places]).astype(jnp.int32)


def halve(value, dim, place):
    first, second = jnp.split(value, 2, dim)
    lower = digit(place) == 0
    return jnp.where(lower, first, second) + swap(jnp.where(lower, second, first), place)


def ordered(own, other, dim, place):
    lower = digit(place) == 0
    return jnp.where(lower, jnp.concatenate([own, other], dim), jnp.concatenate([other, own], dim))


def widen(value, dim, place):
    return ordered(value, swap(value, place), dim, place)


def common_places(count):
    sub_bits = bits_of("sub")
    places = list(range(count))
    if count > sub_bits:
        places.remove(sub_bits)
        places.insert(0, sub_bits)
    return places


def swap_all(values, place):
    width = values[0].shape[-1]
    sent = swap(jnp.concatenate([value.reshape(-1, width) for value in values], 0), place)
    ends = [0]
    for value in values:
        ends.append(ends[-1] + value.size // width)
    return [sent[ends[i] : ends[i + 1]].reshape(value.shape) for i, value in enumerate(values)]


def after(value, token):
    return lax.optimization_barrier((value, token))[0]


def halves(value):
    high = value.astype(jnp.bfloat16)
    return high, (value - high.astype(jnp.float32)).astype(jnp.bfloat16)


def product(left, right, left_dim, right_dim):
    dims = (((left_dim,), (right_dim,)), ((), ()))
    left = jnp.concatenate([left[0], left[0], left[1]], left_dim)
    right = jnp.concatenate([right[0], right[1], right[0]], right_dim)
    return lax.dot_general(left, right, dims, preferred_element_type=jnp.float32)


def first_kernel(where_ref, x_ref, u_ref, v_ref, v_next_ref, keep_ref, send_ref, total, total_next):
    step = pl.program_id(0)

    @pl.when(step == 0)
    def _():
        total[...] = jnp.zeros_like(total)
        total_next[...] = jnp.zeros_like(total_next)

    sides = x_ref.shape[1]
    x, v, v_next = halves(x_ref[...]), halves(v_ref[0]), halves(v_next_ref[0])
    total[...] += product(x, v, 0, 0)
    total_next[:sides] += product(x, v_next, 0, 0)
    total_next[sides:] += product(halves(u_ref[0]), v_next, 0, 0)

    @pl.when(step == pl.num_programs(0) - 1)
    def _():
        where = where_ref[0]
        width = sides // (2 * CHUNKS)
        for ref, side in ((keep_ref, where), (send_ref, 1 - where)):
            for level, each in enumerate((total, total_next)):
                for k in range(CHUNKS):
                    start = pl.multiple_of((2 * k + side) * width, width)
                    at = (level * CHUNKS + k) * width
                    ref[at : at + width, :] = each[pl.ds(start, width), :]
        rank = u_ref.shape[2]
        at = 2 * CHUNKS * width
        for ref, side in ((keep_ref, where), (send_ref, 1 - where)):
            start = pl.multiple_of(sides + side * (rank // 2), rank // 2)
            ref[at:, :] = total_next[pl.ds(start, rank // 2), :]


def slab(rows, rank, level):
    return pl.BlockSpec((1, rows, rank), lambda i, *_: (level, i, 0))


def whole(shape):
    return pl.BlockSpec(shape, lambda *_: (0,) * len(shape))


def shapes(*values):
    return [jax.ShapeDtypeStruct(value, jnp.float32) for value in values]


SMEM = pl.BlockSpec(memory_space=pltpu.SMEM)


def first_sums(where, x, bases_u, bases_v, level):
    rows, sides = x.shape
    rank = bases_u.shape[2]
    block = rows // STEPS
    out = (sides + rank // 2, rank)
    return pl.pallas_call(
        first_kernel,
        grid=(STEPS,),
        in_specs=[
            SMEM,
            pl.BlockSpec((block, sides), lambda i: (i, 0)),
            slab(block, rank, level),
            slab(block, rank, level),
            slab(block, rank, level + 1),
        ],
        out_specs=[whole(out)] * 2,
        out_shape=shapes(out, out),
        scratch_shapes=[pltpu.VMEM((sides, rank), jnp.float32), pltpu.VMEM((sides + rank, rank), jnp.float32)],
        compiler_params=pltpu.CompilerParams(vmem_limit_bytes=60 * MIB),
        cost_estimate=pl.CostEstimate(flops=6 * rows * rank * (2 * sides + rank), bytes_accessed=5 * rows * rank * 4, transcendentals=0),
    )(where, x, bases_u, bases_v, bases_v)


def whole_factors(where, own_ref, partner_ref):
    own, partner = own_ref[...], partner_ref[...]
    first, second = jnp.where(where == 0, own, partner), jnp.where(where == 0, partner, own)
    return [jnp.concatenate([first[k], second[k]], 0) for k in range(2)]


def update(x, left, left_next, factors):
    return x - (product(halves(left), factors[0], 1, 1) + product(halves(left_next), factors[1], 1, 1))


def middle_kernel(chunk, level, where_ref, old_ref, own_ref, partner_ref, u_ref, v_ref, x_ref, keep_ref, send_ref, total, total_next):
    factors = [halves(each) for each in whole_factors(where_ref[0], own_ref, partner_ref)]
    rows, columns = x_ref.shape
    block = rows // STEPS
    sums = None
    for step in range(STEPS):
        at = slice(step * block, (step + 1) * block)
        x = old_ref[at, chunk * columns : (chunk + 1) * columns]
        x = update(x, u_ref[level, at], u_ref[level + 1, at], factors)
        x_ref[at, :] = x
        x = halves(x)
        terms = [product(x, halves(v_ref[level + 2 + k, at]), 0, 0) for k in range(2)]
        sums = terms if sums is None else [a + b for a, b in zip(sums, terms)]
    total[...], total_next[...] = sums
    width = columns // 2
    for ref, side in ((keep_ref, where_ref[1]), (send_ref, 1 - where_ref[1])):
        start = pl.multiple_of(side * width, width)
        ref[:width, :] = total[pl.ds(start, width), :]
        ref[width:, :] = total_next[pl.ds(start, width), :]


VMEM = pl.BlockSpec(memory_space=pltpu.VMEM)
ANY = pl.BlockSpec(memory_space=pl.ANY)


def middle(where, chunk, x, own, partner, bases_u, bases_v, level):
    rows, sides = x.shape
    rank = bases_u.shape[2]
    width = sides // (2 * CHUNKS)
    out = (2 * width, rank)
    return pl.pallas_call(
        functools.partial(middle_kernel, chunk, level),
        in_specs=[SMEM] + [VMEM] * 5,
        out_specs=[VMEM] * 3,
        out_shape=shapes((rows, 2 * width), out, out),
        scratch_shapes=[pltpu.VMEM((2 * width, rank), jnp.float32)] * 2,
        compiler_params=pltpu.CompilerParams(vmem_limit_bytes=MID * MIB),
        cost_estimate=pl.CostEstimate(flops=24 * rows * rank * width * 2, bytes_accessed=4 * rows * rank * 4, transcendentals=0),
    )(where, x, own, partner, bases_u, bases_v)


def last_kernel(chunk, level, where_ref, x_ref, own_ref, partner_ref, u_ref, *refs):
    out_ref, found, sems = refs[-3:]
    factors = [halves(each) for each in whole_factors(where_ref[0], own_ref, partner_ref)]
    rows, columns = x_ref.shape
    block = rows // STEPS
    copies = []
    for step in range(STEPS):
        at = slice(step * block, (step + 1) * block)
        found[at, :] = update(x_ref[at, :], u_ref[level, at], u_ref[level + 1, at], factors)
        place = (pl.ds(step * block, block), pl.ds(chunk * columns, columns))
        copies.append(pltpu.make_async_copy(found.at[pl.ds(step * block, block)], out_ref.at[place], sems.at[step]))
        copies[-1].start()
    for copy in copies:
        copy.wait()


def last(where, chunk, x, own, partner, bases_u, level, into, sides):
    rows = x.shape[0]
    rank = bases_u.shape[2]
    width = sides // (2 * CHUNKS)
    more = [] if into is None else [into]
    return pl.pallas_call(
        functools.partial(last_kernel, chunk, level),
        in_specs=[SMEM] + [VMEM] * 4 + [ANY] * len(more),
        out_specs=ANY,
        out_shape=jax.ShapeDtypeStruct((rows, sides), jnp.float32),
        scratch_shapes=[pltpu.VMEM((rows, 2 * width), jnp.float32), pltpu.SemaphoreType.DMA((STEPS,))],
        input_output_aliases={5: 0} if more else {},
        compiler_params=pltpu.CompilerParams(vmem_limit_bytes=LAST * MIB),
        cost_estimate=pl.CostEstimate(flops=12 * rows * rank * width * 2, bytes_accessed=3 * rows * rank * 4, transcendentals=0),
    )(where, x, own, partner, bases_u, *more)


def gram_kernel(level, u_ref, v_ref, out_ref):
    out_ref[...] = product(halves(u_ref[level]), halves(v_ref[level + 1]), 0, 0)


def gram_term(bases_u, bases_v, level):
    rows, rank = bases_u.shape[1:]
    return pl.pallas_call(
        functools.partial(gram_kernel, level),
        in_specs=[VMEM] * 2,
        out_specs=VMEM,
        out_shape=jax.ShapeDtypeStruct((rank, rank), jnp.float32),
        compiler_params=pltpu.CompilerParams(vmem_limit_bytes=24 * MIB),
        cost_estimate=pl.CostEstimate(flops=6 * rows * rank * rank, bytes_accessed=2 * rows * rank * 4, transcendentals=0),
    )(bases_u, bases_v)


def checkpoint(*values):
    return lax.optimization_barrier(values)


def both_halves(rows):
    return jnp.stack(jnp.split(rows, 2, 1))


class Gather:
    def __init__(self, rows):
        self.values = [both_halves(each) for each in rows]
        self.seen = [[] for _ in rows]

    def begin(self, place, use, extra=()):
        grown = []
        for k in use:
            at = 1 + sum(other > place for other in self.seen[k])
            self.seen[k].append(place)
            grown.append((jnp.expand_dims(self.values[k], at), at))
        sent = [value for value, _ in grown] + list(extra)
        self.held = place, use, grown
        return swap_all(sent, place)

    def end(self, received):
        place, use, grown = self.held
        for k, (value, at), partner in zip(use, grown, received):
            self.values[k] = ordered(value, partner, at, place)
        return received[len(use) :]

    def sides(self, k, place):
        first, second = self.values[k].reshape(2, -1, self.values[k].shape[-1])
        lower = digit(place) == 0
        return jnp.where(lower, first, second), jnp.where(lower, second, first)


def factors_kernel(upper, upper_other, own, sibling, k_own, k_sibling, next_own, next_sibling, gram_own, gram_sibling, out_ref):
    def part(ref):
        return halves(ref[...])

    found = product(part(upper), part(k_own), 1, 1) + product(part(upper_other), part(k_sibling), 1, 1)
    high = halves(found)
    own = halves(own[...] - product(high, part(gram_own), 1, 0))
    sibling = halves(sibling[...] - product(high, part(gram_sibling), 1, 0))
    found_next = product(own, part(next_own), 1, 1) + product(sibling, part(next_sibling), 1, 1)
    count, _, width, _ = out_ref.shape
    for k in range(count):
        out_ref[k, 0] = found[k * width : (k + 1) * width]
        out_ref[k, 1] = found_next[k * width : (k + 1) * width]


def factors(reduced, grams, coupling):
    count, width, rank = reduced[0].shape
    reduced = [value.reshape(count * width, rank) for value in reduced]
    return pl.pallas_call(
        factors_kernel,
        out_shape=jax.ShapeDtypeStruct((count, 2, width, rank), jnp.float32),
        compiler_params=pltpu.CompilerParams(vmem_limit_bytes=16 * MIB),
        cost_estimate=pl.CostEstimate(flops=36 * count * width * rank * rank, bytes_accessed=6 * rank * rank * 4, transcendentals=0),
    )(*reduced, *coupling[0], *coupling[1], *grams)


def upper_kernel(upper, upper_other, own, k_own, k_sibling, gram, factors_ref, own_ref):
    def part(ref):
        return halves(ref[...])

    found = product(part(upper), part(k_own), 1, 1) + product(part(upper_other), part(k_sibling), 1, 1)
    factors_ref[...] = found
    own_ref[...] = own[...] - product(halves(found), part(gram), 1, 0)


def upper_factors(upper, upper_other, own, gram, coupling):
    width, rank = own.shape
    return pl.pallas_call(
        upper_kernel,
        out_shape=shapes((width, rank), (width, rank)),
        compiler_params=pltpu.CompilerParams(vmem_limit_bytes=16 * MIB),
        cost_estimate=pl.CostEstimate(flops=18 * width * rank * rank, bytes_accessed=3 * rank * rank * 4, transcendentals=0),
    )(upper, upper_other, own, *coupling, gram)


def lower_kernel(upper, own, sibling, k_own, k_sibling, out_ref):
    def part(ref):
        return halves(ref[...])

    out_ref[0] = upper[...]
    out_ref[1] = product(part(own), part(k_own), 1, 1) + product(part(sibling), part(k_sibling), 1, 1)


def lower_factors(upper, own, sibling, coupling):
    return pl.pallas_call(
        lower_kernel,
        out_shape=jax.ShapeDtypeStruct((2, *own.shape), jnp.float32),
        compiler_params=pltpu.CompilerParams(vmem_limit_bytes=16 * MIB),
        cost_estimate=pl.CostEstimate(flops=12 * own.size * own.shape[1], bytes_accessed=2 * own.shape[1] ** 2 * 4, transcendentals=0),
    )(upper, own, sibling, *coupling)


def local(right_sides, bases_u, bases_v, couple_first, couple_second, couple_third, couple_fourth):
    couples = (couple_first, couple_second, couple_third, couple_fourth)
    sides, rank = right_sides.shape[1], bases_u.shape[2]
    width = sides // (2 * CHUNKS)
    total_bits = bits_of("sub") + bits_of("rows")
    sibling, sibling_next = total_bits - 2, total_bits - 4
    places, places_next = common_places(sibling), common_places(sibling_next)

    near, far, low = Gather(couples[:2]), Gather(couples[2:3]), Gather(couples[3:])
    inner = places[1:]
    behind = inner[::-1]
    far_order = places_next[::-1]
    far_order.insert(len(far_order) - 1, sibling_next)

    keep, send = first_sums(digits(places[0]), right_sides, bases_u, bases_v, 0)
    sums = keep + swap(send, places[0])
    sums, near.values, far.values = checkpoint(sums, near.values, far.values)
    main, gram = sums[:sides].reshape(2, CHUNKS, width, rank), sums[sides:]
    for step, place in enumerate(inner):
        main = halve(main, 2, place)
        (other,) = near.end(near.begin(behind[step], (0, 1), (gram,)))
        gram = gram + other
        main, gram, near.values, far.values = checkpoint(main, gram, near.values, far.values)
    gram_other, other = near.end(near.begin(sibling, (0,), (gram, main)))
    upper = main[0] + other[0]
    for place in far_order[:-1]:
        far.end(far.begin(place, (0,)))
    term = gram_term(bases_u, bases_v, 2)
    for place in places_next[:-1]:
        term = term + swap(term, place)
    term_other = swap(term, places_next[-1])
    upper_other = swap(upper, sibling + 1)
    pair = jnp.stack([gram, gram_other])
    (pair_partner,) = near.end(near.begin(places[0], (0, 1), (pair,)))
    far.values = after(far.values, upper)
    received = far.begin(far_order[-1], (0,))
    grams = ordered(pair, pair_partner, 1, places[0])
    coupling = near.sides(0, sibling + 1), near.sides(1, sibling)
    found = factors((upper, upper_other, main[1], other[1]), grams, coupling)
    for place in behind[:-1]:
        found = widen(found, 2, place)
    found, term_other, received = checkpoint(found, term_other, received)
    found = [widen(each, 1, place) for each in found for place in behind[-1:]]
    term = term + term_other
    far.end(received)

    where = digits(places[0], places_next[0])
    parts, mains = [], []
    for k, own in enumerate(found):
        part, keep, send = middle(where, k, right_sides, own, swap(own, places[0]), bases_u, bases_v, 0)
        parts.append(part)
        main = (keep + swap(send, places_next[0])).reshape(2, width, rank)
        for place in places_next[1:]:
            main = halve(main, 1, place)
        mains.append(main)
    low.values = after(low.values, mains[LOW])
    for place in places_next[::-1]:
        low.end(low.begin(place, (0,)))
    coupling = far.sides(0, sibling_next + 1), low.sides(0, sibling_next)
    first, done = [], None
    for main in mains:
        other = swap(main[0], sibling_next)
        upper = main[0] + (after(other, done) if first else other)
        first.append(upper_factors(upper, swap(upper, sibling_next + 1), main[1], term, coupling[0]))
        done = first[-1]
    solved, found = None, []
    for part, (upper, own) in zip(parts, first):
        other = swap(own, sibling_next)
        own = lower_factors(upper, own, after(other, done) if found else other, coupling[1])
        found.append(own)
        done = own
    for k, own in enumerate(found):
        for place in places_next[:0:-1]:
            own = widen(own, 1, place)
        partner = swap(own, places_next[0])
        solved = last(digits(places_next[0]), k, parts[k], own, after(partner, solved) if k else partner, bases_u, 2, solved, sides)
    return solved


def solution(mesh):
    placed = (
        P(("rows", "sub"), None),
        P(None, ("rows", "sub"), None),
        P(None, ("rows", "sub"), None),
        P(("rows", "sub"), None),
        P(("rows", "sub"), None),
        P(("rows", "sub"), None),
        P(("rows", "sub"), None),
    )
    return jax.shard_map(
        local, mesh=mesh, in_specs=placed, out_specs=P(("rows", "sub"), None), check_vma=False
    )
```

```python
import functools

import jax
import jax.numpy as jnp
from jax import lax
from jax.experimental import pallas as pl
from jax.experimental.pallas import tpu as pltpu
from jax.sharding import PartitionSpec as P

CHUNKS = 2
STEPS = 2
MIB = 1 << 20
LOW = -1
HOLD = True
FIRST = 50
FIRST_STEPS = 4
LAST_STEPS = 4
MID = 24
LAST = 24


def bits_of(axis):
    return lax.axis_size(axis).bit_length() - 1


def swap(value, place):
    sub_bits = bits_of("sub")
    axis, bit = ("sub", place) if place < sub_bits else ("rows", place - sub_bits)
    return lax.ppermute(value, axis, [(i, i ^ 1 << bit) for i in range(lax.axis_size(axis))])


def digit(place):
    position = lax.axis_index("rows") * lax.axis_size("sub") + lax.axis_index("sub")
    return (position >> place) & 1


def digits(*places):
    return jnp.stack([digit(place) for place in places]).astype(jnp.int32)


def halve(value, dim, place):
    first, second = jnp.split(value, 2, dim)
    lower = digit(place) == 0
    return jnp.where(lower, first, second) + swap(jnp.where(lower, second, first), place)


def ordered(own, other, dim, place):
    lower = digit(place) == 0
    return jnp.where(lower, jnp.concatenate([own, other], dim), jnp.concatenate([other, own], dim))


def widen(value, dim, place):
    return ordered(value, swap(value, place), dim, place)


def common_places(count):
    sub_bits = bits_of("sub")
    places = list(range(count))
    if count > sub_bits:
        places.remove(sub_bits)
        places.insert(0, sub_bits)
    return places


def swap_all(values, place):
    width = values[0].shape[-1]
    sent = swap(jnp.concatenate([value.reshape(-1, width) for value in values], 0), place)
    ends = [0]
    for value in values:
        ends.append(ends[-1] + value.size // width)
    return [sent[ends[i] : ends[i + 1]].reshape(value.shape) for i, value in enumerate(values)]


def after(value, token):
    return lax.optimization_barrier((value, token))[0]


def halves(value):
    high = value.astype(jnp.bfloat16)
    return high, (value - high.astype(jnp.float32)).astype(jnp.bfloat16)


def product(left, right, left_dim, right_dim):
    dims = (((left_dim,), (right_dim,)), ((), ()))
    left = jnp.concatenate([left[0], left[0], left[1]], left_dim)
    right = jnp.concatenate([right[0], right[1], right[0]], right_dim)
    return lax.dot_general(left, right, dims, preferred_element_type=jnp.float32)


def first_kernel(level, where_ref, x_hbm, u_hbm, v_hbm, keep_ref, send_ref, x_ref, u_ref, v_ref, total, total_next, sems):
    rows, sides = x_ref.shape
    rank = u_ref.shape[1]
    block = rows // FIRST_STEPS
    copies = []
    for step in range(FIRST_STEPS):
        at = pl.ds(step * block, block)
        pairs = [
            (x_hbm.at[at], x_ref.at[at]),
            (v_hbm.at[level + 1, at], v_ref.at[1, at]),
            (v_hbm.at[level, at], v_ref.at[0, at]),
            (u_hbm.at[level, at], u_ref.at[at]),
        ]
        copies.append([pltpu.make_async_copy(*pair, sems.at[step, k]) for k, pair in enumerate(pairs)])
        for copy in copies[-1]:
            copy.start()
    for step in range(FIRST_STEPS):
        at = slice(step * block, (step + 1) * block)
        for copy in copies[step]:
            copy.wait()
        x, v, v_next = halves(x_ref[at, :]), halves(v_ref[0, at]), halves(v_ref[1, at])
        terms = product(x, v, 0, 0), product(x, v_next, 0, 0), product(halves(u_ref[at, :]), v_next, 0, 0)
        if step:
            total[...] += terms[0]
            total_next[:sides] += terms[1]
            total_next[sides:] += terms[2]
        else:
            total[...] = terms[0]
            total_next[:sides] = terms[1]
            total_next[sides:] = terms[2]
    where = where_ref[0]
    width = sides // (2 * CHUNKS)
    at = 2 * CHUNKS * width
    for ref, side in ((keep_ref, where), (send_ref, 1 - where)):
        for level, each in enumerate((total, total_next)):
            for k in range(CHUNKS):
                start = pl.multiple_of((2 * k + side) * width, width)
                into = (level * CHUNKS + k) * width
                ref[into : into + width, :] = each[pl.ds(start, width), :]
        start = pl.multiple_of(sides + side * (rank // 2), rank // 2)
        ref[at:, :] = total_next[pl.ds(start, rank // 2), :]


def shapes(*values):
    return [jax.ShapeDtypeStruct(value, jnp.float32) for value in values]


SMEM = pl.BlockSpec(memory_space=pltpu.SMEM)
VMEM = pl.BlockSpec(memory_space=pltpu.VMEM)
ANY = pl.BlockSpec(memory_space=pl.ANY)


def first_sums(where, x, bases_u, bases_v, level):
    rows, sides = x.shape
    rank = bases_u.shape[2]
    out = (sides + rank // 2, rank)
    return pl.pallas_call(
        functools.partial(first_kernel, level),
        in_specs=[SMEM] + [ANY] * 3,
        out_specs=[VMEM] * 2,
        out_shape=shapes(out, out),
        scratch_shapes=[
            pltpu.VMEM((rows, sides), jnp.float32),
            pltpu.VMEM((rows, rank), jnp.float32),
            pltpu.VMEM((2, rows, rank), jnp.float32),
            pltpu.VMEM((sides, rank), jnp.float32),
            pltpu.VMEM((sides + rank, rank), jnp.float32),
            pltpu.SemaphoreType.DMA((FIRST_STEPS, 4)),
        ],
        compiler_params=pltpu.CompilerParams(vmem_limit_bytes=FIRST * MIB),
        cost_estimate=pl.CostEstimate(flops=6 * rows * rank * (2 * sides + rank), bytes_accessed=5 * rows * rank * 4, transcendentals=0),
    )(where, x, bases_u, bases_v)


def whole_factors(where, own_ref, partner_ref):
    own, partner = own_ref[...], partner_ref[...]
    first, second = jnp.where(where == 0, own, partner), jnp.where(where == 0, partner, own)
    return [jnp.concatenate([first[k], second[k]], 0) for k in range(2)]


def update(x, left, left_next, factors):
    return x - (product(halves(left), factors[0], 1, 1) + product(halves(left_next), factors[1], 1, 1))


def middle_kernel(chunk, level, where_ref, old_ref, own_ref, partner_ref, u_ref, v_ref, x_ref, keep_ref, send_ref, total, total_next):
    factors = [halves(each) for each in whole_factors(where_ref[0], own_ref, partner_ref)]
    rows, columns = x_ref.shape
    block = rows // STEPS
    sums = None
    for step in range(STEPS):
        at = slice(step * block, (step + 1) * block)
        x = old_ref[at, chunk * columns : (chunk + 1) * columns]
        x = update(x, u_ref[level, at], u_ref[level + 1, at], factors)
        x_ref[at, :] = x
        x = halves(x)
        terms = [product(x, halves(v_ref[level + 2 + k, at]), 0, 0) for k in range(2)]
        sums = terms if sums is None else [a + b for a, b in zip(sums, terms)]
    total[...], total_next[...] = sums
    width = columns // 2
    for ref, side in ((keep_ref, where_ref[1]), (send_ref, 1 - where_ref[1])):
        start = pl.multiple_of(side * width, width)
        ref[:width, :] = total[pl.ds(start, width), :]
        ref[width:, :] = total_next[pl.ds(start, width), :]


def middle(where, chunk, x, own, partner, bases_u, bases_v, level):
    rows, sides = x.shape
    rank = bases_u.shape[2]
    width = sides // (2 * CHUNKS)
    out = (2 * width, rank)
    return pl.pallas_call(
        functools.partial(middle_kernel, chunk, level),
        in_specs=[SMEM] + [VMEM] * 5,
        out_specs=[VMEM] * 3,
        out_shape=shapes((rows, 2 * width), out, out),
        scratch_shapes=[pltpu.VMEM((2 * width, rank), jnp.float32)] * 2,
        compiler_params=pltpu.CompilerParams(vmem_limit_bytes=MID * MIB),
        cost_estimate=pl.CostEstimate(flops=24 * rows * rank * width * 2, bytes_accessed=4 * rows * rank * 4, transcendentals=0),
    )(where, x, own, partner, bases_u, bases_v)


def last_kernel(chunk, level, where_ref, x_ref, own_ref, partner_ref, u_ref, *refs):
    out_ref, found, sems = refs[-3:]
    factors = [halves(each) for each in whole_factors(where_ref[0], own_ref, partner_ref)]
    rows, columns = x_ref.shape
    block = rows // LAST_STEPS
    copies = []
    for step in range(LAST_STEPS):
        at = slice(step * block, (step + 1) * block)
        found[at, :] = update(x_ref[at, :], u_ref[level, at], u_ref[level + 1, at], factors)
        place = (pl.ds(step * block, block), pl.ds(chunk * columns, columns))
        copies.append(pltpu.make_async_copy(found.at[pl.ds(step * block, block)], out_ref.at[place], sems.at[step]))
        copies[-1].start()
    for copy in copies:
        copy.wait()


def last(where, chunk, x, own, partner, bases_u, level, into, sides):
    rows = x.shape[0]
    rank = bases_u.shape[2]
    width = sides // (2 * CHUNKS)
    more = [] if into is None else [into]
    return pl.pallas_call(
        functools.partial(last_kernel, chunk, level),
        in_specs=[SMEM] + [VMEM] * 4 + [ANY] * len(more),
        out_specs=ANY,
        out_shape=jax.ShapeDtypeStruct((rows, sides), jnp.float32),
        scratch_shapes=[pltpu.VMEM((rows, 2 * width), jnp.float32), pltpu.SemaphoreType.DMA((LAST_STEPS,))],
        input_output_aliases={5: 0} if more else {},
        compiler_params=pltpu.CompilerParams(vmem_limit_bytes=LAST * MIB),
        cost_estimate=pl.CostEstimate(flops=12 * rows * rank * width * 2, bytes_accessed=3 * rows * rank * 4, transcendentals=0),
    )(where, x, own, partner, bases_u, *more)


def gram_kernel(level, u_ref, v_ref, out_ref):
    out_ref[...] = product(halves(u_ref[level]), halves(v_ref[level + 1]), 0, 0)


def gram_term(bases_u, bases_v, level):
    rows, rank = bases_u.shape[1:]
    return pl.pallas_call(
        functools.partial(gram_kernel, level),
        in_specs=[VMEM] * 2,
        out_specs=VMEM,
        out_shape=jax.ShapeDtypeStruct((rank, rank), jnp.float32),
        compiler_params=pltpu.CompilerParams(vmem_limit_bytes=24 * MIB),
        cost_estimate=pl.CostEstimate(flops=6 * rows * rank * rank, bytes_accessed=2 * rows * rank * 4, transcendentals=0),
    )(bases_u, bases_v)


def checkpoint(*values):
    return lax.optimization_barrier(values)


def both_halves(rows):
    return jnp.stack(jnp.split(rows, 2, 1))


class Gather:
    def __init__(self, rows):
        self.values = [both_halves(each) for each in rows]
        self.seen = [[] for _ in rows]

    def begin(self, place, use, extra=()):
        grown = []
        for k in use:
            at = 1 + sum(other > place for other in self.seen[k])
            self.seen[k].append(place)
            grown.append((jnp.expand_dims(self.values[k], at), at))
        sent = [value for value, _ in grown] + list(extra)
        self.held = place, use, grown
        return swap_all(sent, place)

    def end(self, received):
        place, use, grown = self.held
        for k, (value, at), partner in zip(use, grown, received):
            self.values[k] = ordered(value, partner, at, place)
        return received[len(use) :]

    def sides(self, k, place):
        first, second = self.values[k].reshape(2, -1, self.values[k].shape[-1])
        lower = digit(place) == 0
        return jnp.where(lower, first, second), jnp.where(lower, second, first)


def factors_kernel(upper, upper_other, own, sibling, k_own, k_sibling, next_own, next_sibling, gram_own, gram_sibling, out_ref):
    def part(ref):
        return halves(ref[...])

    found = product(part(upper), part(k_own), 1, 1) + product(part(upper_other), part(k_sibling), 1, 1)
    high = halves(found)
    own = halves(own[...] - product(high, part(gram_own), 1, 0))
    sibling = halves(sibling[...] - product(high, part(gram_sibling), 1, 0))
    found_next = product(own, part(next_own), 1, 1) + product(sibling, part(next_sibling), 1, 1)
    count, _, width, _ = out_ref.shape
    for k in range(count):
        out_ref[k, 0] = found[k * width : (k + 1) * width]
        out_ref[k, 1] = found_next[k * width : (k + 1) * width]


def factors(reduced, grams, coupling):
    count, width, rank = reduced[0].shape
    reduced = [value.reshape(count * width, rank) for value in reduced]
    return pl.pallas_call(
        factors_kernel,
        out_shape=jax.ShapeDtypeStruct((count, 2, width, rank), jnp.float32),
        compiler_params=pltpu.CompilerParams(vmem_limit_bytes=16 * MIB),
        cost_estimate=pl.CostEstimate(flops=36 * count * width * rank * rank, bytes_accessed=6 * rank * rank * 4, transcendentals=0),
    )(*reduced, *coupling[0], *coupling[1], *grams)


def upper_kernel(upper, upper_other, own, k_own, k_sibling, gram, factors_ref, own_ref):
    def part(ref):
        return halves(ref[...])

    found = product(part(upper), part(k_own), 1, 1) + product(part(upper_other), part(k_sibling), 1, 1)
    factors_ref[...] = found
    own_ref[...] = own[...] - product(halves(found), part(gram), 1, 0)


def upper_factors(upper, upper_other, own, gram, coupling):
    width, rank = own.shape
    return pl.pallas_call(
        upper_kernel,
        out_shape=shapes((width, rank), (width, rank)),
        compiler_params=pltpu.CompilerParams(vmem_limit_bytes=16 * MIB),
        cost_estimate=pl.CostEstimate(flops=18 * width * rank * rank, bytes_accessed=3 * rank * rank * 4, transcendentals=0),
    )(upper, upper_other, own, *coupling, gram)


def lower_kernel(upper, own, sibling, k_own, k_sibling, out_ref):
    def part(ref):
        return halves(ref[...])

    out_ref[0] = upper[...]
    out_ref[1] = product(part(own), part(k_own), 1, 1) + product(part(sibling), part(k_sibling), 1, 1)


def lower_factors(upper, own, sibling, coupling):
    return pl.pallas_call(
        lower_kernel,
        out_shape=jax.ShapeDtypeStruct((2, *own.shape), jnp.float32),
        compiler_params=pltpu.CompilerParams(vmem_limit_bytes=16 * MIB),
        cost_estimate=pl.CostEstimate(flops=12 * own.size * own.shape[1], bytes_accessed=2 * own.shape[1] ** 2 * 4, transcendentals=0),
    )(upper, own, sibling, *coupling)


def local(right_sides, bases_u, bases_v, couple_first, couple_second, couple_third, couple_fourth):
    couples = (couple_first, couple_second, couple_third, couple_fourth)
    sides, rank = right_sides.shape[1], bases_u.shape[2]
    width = sides // (2 * CHUNKS)
    total_bits = bits_of("sub") + bits_of("rows")
    sibling, sibling_next = total_bits - 2, total_bits - 4
    places, places_next = common_places(sibling), common_places(sibling_next)

    near, far, low = Gather(couples[:2]), Gather(couples[2:3]), Gather(couples[3:])
    inner = places[1:]
    behind = inner[::-1]
    far_order = places_next[::-1]
    far_order.insert(len(far_order) - 1, sibling_next)

    keep, send = first_sums(digits(places[0]), right_sides, bases_u, bases_v, 0)
    sums = keep + swap(send, places[0])
    sums, near.values, far.values = checkpoint(sums, near.values, far.values)
    if HOLD:
        right_sides, bases_u, bases_v = after((right_sides, bases_u, bases_v), send)
    main, gram = sums[:sides].reshape(2, CHUNKS, width, rank), sums[sides:]
    for step, place in enumerate(inner):
        main = halve(main, 2, place)
        (other,) = near.end(near.begin(behind[step], (0, 1), (gram,)))
        gram = gram + other
        main, gram, near.values, far.values = checkpoint(main, gram, near.values, far.values)
    gram_other, other = near.end(near.begin(sibling, (0,), (gram, main)))
    upper = main[0] + other[0]
    for place in far_order[:-1]:
        far.end(far.begin(place, (0,)))
    term = gram_term(bases_u, bases_v, 2)
    for place in places_next[:-1]:
        term = term + swap(term, place)
    term_other = swap(term, places_next[-1])
    upper_other = swap(upper, sibling + 1)
    pair = jnp.stack([gram, gram_other])
    (pair_partner,) = near.end(near.begin(places[0], (0, 1), (pair,)))
    far.values = after(far.values, upper)
    received = far.begin(far_order[-1], (0,))
    grams = ordered(pair, pair_partner, 1, places[0])
    coupling = near.sides(0, sibling + 1), near.sides(1, sibling)
    found = factors((upper, upper_other, main[1], other[1]), grams, coupling)
    for place in behind[:-1]:
        found = widen(found, 2, place)
    found, term_other, received = checkpoint(found, term_other, received)
    found = [widen(each, 1, place) for each in found for place in behind[-1:]]
    term = term + term_other
    far.end(received)

    where = digits(places[0], places_next[0])
    parts, mains = [], []
    for k, own in enumerate(found):
        part, keep, send = middle(where, k, right_sides, own, swap(own, places[0]), bases_u, bases_v, 0)
        parts.append(part)
        main = (keep + swap(send, places_next[0])).reshape(2, width, rank)
        for place in places_next[1:]:
            main = halve(main, 1, place)
        mains.append(main)
    low.values = after(low.values, mains[LOW])
    for place in places_next[::-1]:
        low.end(low.begin(place, (0,)))
    coupling = far.sides(0, sibling_next + 1), low.sides(0, sibling_next)
    first, done = [], None
    for main in mains:
        other = swap(main[0], sibling_next)
        upper = main[0] + (after(other, done) if first else other)
        first.append(upper_factors(upper, swap(upper, sibling_next + 1), main[1], term, coupling[0]))
        done = first[-1]
    solved, found = None, []
    for part, (upper, own) in zip(parts, first):
        other = swap(own, sibling_next)
        own = lower_factors(upper, own, after(other, done) if found else other, coupling[1])
        found.append(own)
        done = own
    for k, own in enumerate(found):
        for place in places_next[:0:-1]:
            own = widen(own, 1, place)
        partner = swap(own, places_next[0])
        solved = last(digits(places_next[0]), k, parts[k], own, after(partner, solved) if k else partner, bases_u, 2, solved, sides)
    return solved


def solution(mesh):
    placed = (
        P(("rows", "sub"), None),
        P(None, ("rows", "sub"), None),
        P(None, ("rows", "sub"), None),
        P(("rows", "sub"), None),
        P(("rows", "sub"), None),
        P(("rows", "sub"), None),
        P(("rows", "sub"), None),
    )
    return jax.shard_map(
        local, mesh=mesh, in_specs=placed, out_specs=P(("rows", "sub"), None), check_vma=False
    )
```

```python
import functools

import jax
import jax.numpy as jnp
from jax import lax
from jax.experimental import pallas as pl
from jax.experimental.pallas import tpu as pltpu
from jax.sharding import PartitionSpec as P

CHUNKS = 2
STEPS = 2
MIB = 1 << 20
LOW = -1
HOLD = True
FIRST = 50
FIRST_STEPS = 2
LAST_STEPS = 4
MID = 24
LAST = 24


def bits_of(axis):
    return lax.axis_size(axis).bit_length() - 1


def swap(value, place):
    sub_bits = bits_of("sub")
    axis, bit = ("sub", place) if place < sub_bits else ("rows", place - sub_bits)
    return lax.ppermute(value, axis, [(i, i ^ 1 << bit) for i in range(lax.axis_size(axis))])


def digit(place):
    position = lax.axis_index("rows") * lax.axis_size("sub") + lax.axis_index("sub")
    return (position >> place) & 1


def digits(*places):
    return jnp.stack([digit(place) for place in places]).astype(jnp.int32)


def halve(value, dim, place):
    first, second = jnp.split(value, 2, dim)
    lower = digit(place) == 0
    return jnp.where(lower, first, second) + swap(jnp.where(lower, second, first), place)


def ordered(own, other, dim, place):
    lower = digit(place) == 0
    return jnp.where(lower, jnp.concatenate([own, other], dim), jnp.concatenate([other, own], dim))


def widen(value, dim, place):
    return ordered(value, swap(value, place), dim, place)


def common_places(count):
    sub_bits = bits_of("sub")
    places = list(range(count))
    if count > sub_bits:
        places.remove(sub_bits)
        places.insert(0, sub_bits)
    return places


def swap_all(values, place):
    width = values[0].shape[-1]
    sent = swap(jnp.concatenate([value.reshape(-1, width) for value in values], 0), place)
    ends = [0]
    for value in values:
        ends.append(ends[-1] + value.size // width)
    return [sent[ends[i] : ends[i + 1]].reshape(value.shape) for i, value in enumerate(values)]


def after(value, token):
    return lax.optimization_barrier((value, token))[0]


def halves(value):
    high = value.astype(jnp.bfloat16)
    return high, (value - high.astype(jnp.float32)).astype(jnp.bfloat16)


def product(left, right, left_dim, right_dim):
    dims = (((left_dim,), (right_dim,)), ((), ()))
    left = jnp.concatenate([left[0], left[0], left[1]], left_dim)
    right = jnp.concatenate([right[0], right[1], right[0]], right_dim)
    return lax.dot_general(left, right, dims, preferred_element_type=jnp.float32)


def first_kernel(level, where_ref, x_hbm, u_hbm, v_hbm, keep_ref, send_ref, x_ref, u_ref, v_ref, total, total_next, sems):
    rows, sides = x_ref.shape
    rank = u_ref.shape[1]
    block = rows // FIRST_STEPS
    copies = []
    for step in range(FIRST_STEPS):
        at = pl.ds(step * block, block)
        pairs = [
            (x_hbm.at[at], x_ref.at[at]),
            (v_hbm.at[level + 1, at], v_ref.at[1, at]),
            (v_hbm.at[level, at], v_ref.at[0, at]),
            (u_hbm.at[level, at], u_ref.at[at]),
        ]
        copies.append([pltpu.make_async_copy(*pair, sems.at[step, k]) for k, pair in enumerate(pairs)])
        for copy in copies[-1]:
            copy.start()
    for step in range(FIRST_STEPS):
        at = slice(step * block, (step + 1) * block)
        for copy in copies[step]:
            copy.wait()
        x, v, v_next = halves(x_ref[at, :]), halves(v_ref[0, at]), halves(v_ref[1, at])
        terms = product(x, v, 0, 0), product(x, v_next, 0, 0), product(halves(u_ref[at, :]), v_next, 0, 0)
        if step:
            total[...] += terms[0]
            total_next[:sides] += terms[1]
            total_next[sides:] += terms[2]
        else:
            total[...] = terms[0]
            total_next[:sides] = terms[1]
            total_next[sides:] = terms[2]
    where = where_ref[0]
    width = sides // (2 * CHUNKS)
    at = 2 * CHUNKS * width
    for ref, side in ((keep_ref, where), (send_ref, 1 - where)):
        for level, each in enumerate((total, total_next)):
            for k in range(CHUNKS):
                start = pl.multiple_of((2 * k + side) * width, width)
                into = (level * CHUNKS + k) * width
                ref[into : into + width, :] = each[pl.ds(start, width), :]
        start = pl.multiple_of(sides + side * (rank // 2), rank // 2)
        ref[at:, :] = total_next[pl.ds(start, rank // 2), :]


def shapes(*values):
    return [jax.ShapeDtypeStruct(value, jnp.float32) for value in values]


SMEM = pl.BlockSpec(memory_space=pltpu.SMEM)
VMEM = pl.BlockSpec(memory_space=pltpu.VMEM)
ANY = pl.BlockSpec(memory_space=pl.ANY)


def first_sums(where, x, bases_u, bases_v, level):
    rows, sides = x.shape
    rank = bases_u.shape[2]
    out = (sides + rank // 2, rank)
    return pl.pallas_call(
        functools.partial(first_kernel, level),
        in_specs=[SMEM] + [ANY] * 3,
        out_specs=[VMEM] * 2,
        out_shape=shapes(out, out),
        scratch_shapes=[
            pltpu.VMEM((rows, sides), jnp.float32),
            pltpu.VMEM((rows, rank), jnp.float32),
            pltpu.VMEM((2, rows, rank), jnp.float32),
            pltpu.VMEM((sides, rank), jnp.float32),
            pltpu.VMEM((sides + rank, rank), jnp.float32),
            pltpu.SemaphoreType.DMA((FIRST_STEPS, 4)),
        ],
        compiler_params=pltpu.CompilerParams(vmem_limit_bytes=FIRST * MIB),
        cost_estimate=pl.CostEstimate(flops=6 * rows * rank * (2 * sides + rank), bytes_accessed=5 * rows * rank * 4, transcendentals=0),
    )(where, x, bases_u, bases_v)


def whole_factors(where, own_ref, partner_ref):
    own, partner = own_ref[...], partner_ref[...]
    first, second = jnp.where(where == 0, own, partner), jnp.where(where == 0, partner, own)
    return [jnp.concatenate([first[k], second[k]], 0) for k in range(2)]


def update(x, left, left_next, factors):
    return x - (product(halves(left), factors[0], 1, 1) + product(halves(left_next), factors[1], 1, 1))


def middle_kernel(chunk, level, where_ref, old_ref, own_ref, partner_ref, u_ref, v_ref, x_ref, keep_ref, send_ref, total, total_next):
    factors = [halves(each) for each in whole_factors(where_ref[0], own_ref, partner_ref)]
    rows, columns = x_ref.shape
    block = rows // STEPS
    sums = None
    for step in range(STEPS):
        at = slice(step * block, (step + 1) * block)
        x = old_ref[at, chunk * columns : (chunk + 1) * columns]
        x = update(x, u_ref[level, at], u_ref[level + 1, at], factors)
        x_ref[at, :] = x
        x = halves(x)
        terms = [product(x, halves(v_ref[level + 2 + k, at]), 0, 0) for k in range(2)]
        sums = terms if sums is None else [a + b for a, b in zip(sums, terms)]
    total[...], total_next[...] = sums
    width = columns // 2
    for ref, side in ((keep_ref, where_ref[1]), (send_ref, 1 - where_ref[1])):
        start = pl.multiple_of(side * width, width)
        ref[:width, :] = total[pl.ds(start, width), :]
        ref[width:, :] = total_next[pl.ds(start, width), :]


def middle(where, chunk, x, own, partner, bases_u, bases_v, level):
    rows, sides = x.shape
    rank = bases_u.shape[2]
    width = sides // (2 * CHUNKS)
    out = (2 * width, rank)
    return pl.pallas_call(
        functools.partial(middle_kernel, chunk, level),
        in_specs=[SMEM] + [VMEM] * 5,
        out_specs=[VMEM] * 3,
        out_shape=shapes((rows, 2 * width), out, out),
        scratch_shapes=[pltpu.VMEM((2 * width, rank), jnp.float32)] * 2,
        compiler_params=pltpu.CompilerParams(vmem_limit_bytes=MID * MIB),
        cost_estimate=pl.CostEstimate(flops=24 * rows * rank * width * 2, bytes_accessed=4 * rows * rank * 4, transcendentals=0),
    )(where, x, own, partner, bases_u, bases_v)


def last_kernel(chunk, level, where_ref, x_ref, own_ref, partner_ref, u_ref, *refs):
    out_ref, found, sems = refs[-3:]
    factors = [halves(each) for each in whole_factors(where_ref[0], own_ref, partner_ref)]
    rows, columns = x_ref.shape
    block = rows // LAST_STEPS
    copies = []
    for step in range(LAST_STEPS):
        at = slice(step * block, (step + 1) * block)
        found[at, :] = update(x_ref[at, :], u_ref[level, at], u_ref[level + 1, at], factors)
        place = (pl.ds(step * block, block), pl.ds(chunk * columns, columns))
        copies.append(pltpu.make_async_copy(found.at[pl.ds(step * block, block)], out_ref.at[place], sems.at[step]))
        copies[-1].start()
    for copy in copies:
        copy.wait()


def last(where, chunk, x, own, partner, bases_u, level, into, sides):
    rows = x.shape[0]
    rank = bases_u.shape[2]
    width = sides // (2 * CHUNKS)
    more = [] if into is None else [into]
    return pl.pallas_call(
        functools.partial(last_kernel, chunk, level),
        in_specs=[SMEM] + [VMEM] * 4 + [ANY] * len(more),
        out_specs=ANY,
        out_shape=jax.ShapeDtypeStruct((rows, sides), jnp.float32),
        scratch_shapes=[pltpu.VMEM((rows, 2 * width), jnp.float32), pltpu.SemaphoreType.DMA((LAST_STEPS,))],
        input_output_aliases={5: 0} if more else {},
        compiler_params=pltpu.CompilerParams(vmem_limit_bytes=LAST * MIB),
        cost_estimate=pl.CostEstimate(flops=12 * rows * rank * width * 2, bytes_accessed=3 * rows * rank * 4, transcendentals=0),
    )(where, x, own, partner, bases_u, *more)


def gram_kernel(level, u_ref, v_ref, out_ref):
    out_ref[...] = product(halves(u_ref[level]), halves(v_ref[level + 1]), 0, 0)


def gram_term(bases_u, bases_v, level):
    rows, rank = bases_u.shape[1:]
    return pl.pallas_call(
        functools.partial(gram_kernel, level),
        in_specs=[VMEM] * 2,
        out_specs=VMEM,
        out_shape=jax.ShapeDtypeStruct((rank, rank), jnp.float32),
        compiler_params=pltpu.CompilerParams(vmem_limit_bytes=24 * MIB),
        cost_estimate=pl.CostEstimate(flops=6 * rows * rank * rank, bytes_accessed=2 * rows * rank * 4, transcendentals=0),
    )(bases_u, bases_v)


def checkpoint(*values):
    return lax.optimization_barrier(values)


def both_halves(rows):
    return jnp.stack(jnp.split(rows, 2, 1))


class Gather:
    def __init__(self, rows):
        self.values = [both_halves(each) for each in rows]
        self.seen = [[] for _ in rows]

    def begin(self, place, use, extra=()):
        grown = []
        for k in use:
            at = 1 + sum(other > place for other in self.seen[k])
            self.seen[k].append(place)
            grown.append((jnp.expand_dims(self.values[k], at), at))
        sent = [value for value, _ in grown] + list(extra)
        self.held = place, use, grown
        return swap_all(sent, place)

    def end(self, received):
        place, use, grown = self.held
        for k, (value, at), partner in zip(use, grown, received):
            self.values[k] = ordered(value, partner, at, place)
        return received[len(use) :]

    def sides(self, k, place):
        first, second = self.values[k].reshape(2, -1, self.values[k].shape[-1])
        lower = digit(place) == 0
        return jnp.where(lower, first, second), jnp.where(lower, second, first)


def factors_kernel(upper, upper_other, own, sibling, k_own, k_sibling, next_own, next_sibling, gram_own, gram_sibling, out_ref):
    def part(ref):
        return halves(ref[...])

    found = product(part(upper), part(k_own), 1, 1) + product(part(upper_other), part(k_sibling), 1, 1)
    high = halves(found)
    own = halves(own[...] - product(high, part(gram_own), 1, 0))
    sibling = halves(sibling[...] - product(high, part(gram_sibling), 1, 0))
    found_next = product(own, part(next_own), 1, 1) + product(sibling, part(next_sibling), 1, 1)
    count, _, width, _ = out_ref.shape
    for k in range(count):
        out_ref[k, 0] = found[k * width : (k + 1) * width]
        out_ref[k, 1] = found_next[k * width : (k + 1) * width]


def factors(reduced, grams, coupling):
    count, width, rank = reduced[0].shape
    reduced = [value.reshape(count * width, rank) for value in reduced]
    return pl.pallas_call(
        factors_kernel,
        out_shape=jax.ShapeDtypeStruct((count, 2, width, rank), jnp.float32),
        compiler_params=pltpu.CompilerParams(vmem_limit_bytes=16 * MIB),
        cost_estimate=pl.CostEstimate(flops=36 * count * width * rank * rank, bytes_accessed=6 * rank * rank * 4, transcendentals=0),
    )(*reduced, *coupling[0], *coupling[1], *grams)


def upper_kernel(upper, upper_other, own, k_own, k_sibling, gram, factors_ref, own_ref):
    def part(ref):
        return halves(ref[...])

    found = product(part(upper), part(k_own), 1, 1) + product(part(upper_other), part(k_sibling), 1, 1)
    factors_ref[...] = found
    own_ref[...] = own[...] - product(halves(found), part(gram), 1, 0)


def upper_factors(upper, upper_other, own, gram, coupling):
    width, rank = own.shape
    return pl.pallas_call(
        upper_kernel,
        out_shape=shapes((width, rank), (width, rank)),
        compiler_params=pltpu.CompilerParams(vmem_limit_bytes=16 * MIB),
        cost_estimate=pl.CostEstimate(flops=18 * width * rank * rank, bytes_accessed=3 * rank * rank * 4, transcendentals=0),
    )(upper, upper_other, own, *coupling, gram)


def lower_kernel(upper, own, sibling, k_own, k_sibling, out_ref):
    def part(ref):
        return halves(ref[...])

    out_ref[0] = upper[...]
    out_ref[1] = product(part(own), part(k_own), 1, 1) + product(part(sibling), part(k_sibling), 1, 1)


def lower_factors(upper, own, sibling, coupling):
    return pl.pallas_call(
        lower_kernel,
        out_shape=jax.ShapeDtypeStruct((2, *own.shape), jnp.float32),
        compiler_params=pltpu.CompilerParams(vmem_limit_bytes=16 * MIB),
        cost_estimate=pl.CostEstimate(flops=12 * own.size * own.shape[1], bytes_accessed=2 * own.shape[1] ** 2 * 4, transcendentals=0),
    )(upper, own, sibling, *coupling)


def local(right_sides, bases_u, bases_v, couple_first, couple_second, couple_third, couple_fourth):
    couples = (couple_first, couple_second, couple_third, couple_fourth)
    sides, rank = right_sides.shape[1], bases_u.shape[2]
    width = sides // (2 * CHUNKS)
    total_bits = bits_of("sub") + bits_of("rows")
    sibling, sibling_next = total_bits - 2, total_bits - 4
    places, places_next = common_places(sibling), common_places(sibling_next)

    near, far, low = Gather(couples[:2]), Gather(couples[2:3]), Gather(couples[3:])
    inner = places[1:]
    behind = inner[::-1]
    far_order = places_next[::-1]
    far_order.insert(len(far_order) - 1, sibling_next)

    keep, send = first_sums(digits(places[0]), right_sides, bases_u, bases_v, 0)
    sums = keep + swap(send, places[0])
    sums, near.values, far.values = checkpoint(sums, near.values, far.values)
    if HOLD:
        right_sides, bases_u, bases_v = after((right_sides, bases_u, bases_v), send)
    main, gram = sums[:sides].reshape(2, CHUNKS, width, rank), sums[sides:]
    for step, place in enumerate(inner):
        main = halve(main, 2, place)
        (other,) = near.end(near.begin(behind[step], (0, 1), (gram,)))
        gram = gram + other
        main, gram, near.values, far.values = checkpoint(main, gram, near.values, far.values)
    gram_other, other = near.end(near.begin(sibling, (0,), (gram, main)))
    upper = main[0] + other[0]
    for place in far_order[:-1]:
        far.end(far.begin(place, (0,)))
    term = gram_term(bases_u, bases_v, 2)
    for place in places_next[:-1]:
        term = term + swap(term, place)
    term_other = swap(term, places_next[-1])
    upper_other = swap(upper, sibling + 1)
    pair = jnp.stack([gram, gram_other])
    (pair_partner,) = near.end(near.begin(places[0], (0, 1), (pair,)))
    far.values = after(far.values, upper)
    received = far.begin(far_order[-1], (0,))
    grams = ordered(pair, pair_partner, 1, places[0])
    coupling = near.sides(0, sibling + 1), near.sides(1, sibling)
    found = factors((upper, upper_other, main[1], other[1]), grams, coupling)
    for place in behind[:-1]:
        found = widen(found, 2, place)
    found, term_other, received = checkpoint(found, term_other, received)
    found = [widen(each, 1, place) for each in found for place in behind[-1:]]
    term = term + term_other
    far.end(received)

    where = digits(places[0], places_next[0])
    parts, mains = [], []
    for k, own in enumerate(found):
        part, keep, send = middle(where, k, right_sides, own, swap(own, places[0]), bases_u, bases_v, 0)
        parts.append(part)
        main = (keep + swap(send, places_next[0])).reshape(2, width, rank)
        for place in places_next[1:]:
            main = halve(main, 1, place)
        mains.append(main)
    low.values = after(low.values, mains[LOW])
    for place in places_next[::-1]:
        low.end(low.begin(place, (0,)))
    coupling = far.sides(0, sibling_next + 1), low.sides(0, sibling_next)
    first, done = [], None
    for main in mains:
        other = swap(main[0], sibling_next)
        upper = main[0] + (after(other, done) if first else other)
        first.append(upper_factors(upper, swap(upper, sibling_next + 1), main[1], term, coupling[0]))
        done = first[-1]
    solved, found = None, []
    for part, (upper, own) in zip(parts, first):
        other = swap(own, sibling_next)
        own = lower_factors(upper, own, after(other, done) if found else other, coupling[1])
        found.append(own)
        done = own
    for k, own in enumerate(found):
        for place in places_next[:0:-1]:
            own = widen(own, 1, place)
        partner = swap(own, places_next[0])
        solved = last(digits(places_next[0]), k, parts[k], own, after(partner, solved) if k else partner, bases_u, 2, solved, sides)
    return solved


def solution(mesh):
    placed = (
        P(("rows", "sub"), None),
        P(None, ("rows", "sub"), None),
        P(None, ("rows", "sub"), None),
        P(("rows", "sub"), None),
        P(("rows", "sub"), None),
        P(("rows", "sub"), None),
        P(("rows", "sub"), None),
    )
    return jax.shard_map(
        local, mesh=mesh, in_specs=placed, out_specs=P(("rows", "sub"), None), check_vma=False
    )
```
